32 devices in a mesh: blk: 8 (over z, y), dp: 4 (over x, core).
Axes of the slice: x: 2, y: 2, z: 4, core: 2. Of those that a mesh axis runs over, the one named last changes fastest.
Arguments:
- tokens: bfloat16 [12288, 4096], P(('blk', 'dp')), may hold values from -6 to 6
- grad_k: bfloat16 [12288, 1024], P(('blk', 'dp')), may hold values from -6 to 6
- adapter_a: bfloat16 [4096, 192], P('blk'), may hold values from -0.09375 to 0.09375
- adapter_b: bfloat16 [192, 1024], P('blk'), may hold values from -0.1875 to 0.1875
Outputs:
- grad_a: float32 [4096, 192], P('blk')
- grad_b: float32 [192, 1024], P('blk')
The draws below stay inside these ranges and needn't reach their ends.
All inputs are finite; a program needn't handle non-finite values.
Results may differ from the reference program's by a relative error of at most 0.003.
Values may be sent and summed in bfloat16 or wider, within the bound.
A program may use at most 64 MiB of HBM per device.

```python
import jax
import jax.numpy as jnp
from jax import lax

D = 4096
R = 192
TOK_DEV = 384
KW = 1024
TOKENS = 12288
N_BLK = 8


def spiked(values, stream_key, source, target, blocks, factor):
    def block_of(position):
        return (jnp.arange(values.shape[position]) // (values.shape[position] // blocks)).reshape((-1,) + (1,) * (values.ndim - 1 - position))

    one_side = jax.random.permutation(stream_key, blocks)[block_of(target)]
    far = (block_of(target) + blocks // 2) % blocks
    return jnp.where((block_of(source) == one_side) | (block_of(source) == far), factor * values, values)


def steps_of(own_key, dims, split, smallest, high):
    level, own = 1.0, jax.random.fold_in(own_key, 6)
    for axis_at, parts in split:
        draws = jnp.exp(jax.random.uniform(jax.random.fold_in(own, axis_at), (parts,), jnp.float32, smallest / len(split), high / len(split)))
        level = level * jnp.repeat(draws, dims[axis_at] // parts).reshape([-1 if axis == axis_at else 1 for axis in range(len(dims))])
    return level


def normal_values(key, extent, scale, bound, split=(), kind=jnp.bfloat16):
    result = scale * jax.random.normal(key, extent, jnp.float32)
    if split:
        result = result * steps_of(key, extent, split, -0.22, 0.18)
    return jnp.clip(result, -bound, bound).astype(kind)


def noise_with(rng, extent, deviation, limit, split, heavy, dtype=jnp.bfloat16):
    array = deviation * jax.random.normal(rng, extent, jnp.float32)
    if split:
        array = array * steps_of(rng, extent, split, -0.22, 0.18)
    return jnp.clip(spiked(array, jax.random.fold_in(rng, 3), *heavy), -limit, limit).astype(dtype)


def setup_inputs(seed: int = 0) -> dict:
    key_of = jax.random.split(jax.random.key(seed), 5)
    return {
        "tokens": noise_with(key_of[0], (TOKENS, D), 1.0, 6.0, ((0, 32),), (0, 1, 32, 2.75)),
        "grad_k": normal_values(key_of[1], (TOKENS, KW), 1.0, 6.0, ((0, 32),)),
        "adapter_a": normal_values(key_of[2], (D, R), D ** -0.5, 0.09375, ((0, 8),)),
        "adapter_b": normal_values(key_of[3], (R, KW), KW ** -0.5, 0.1875, ((0, 8),)),
    }


def reference(tokens, grad_k, adapter_a, adapter_b):
    rows = TOK_DEV * N_BLK
    blocks = TOKENS // rows
    token_blocks = tokens.reshape(blocks, rows, D)
    grad_blocks = grad_k.reshape(blocks, rows, KW)
    factor_a = adapter_a.astype(jnp.float32)
    factor_b = adapter_b.astype(jnp.float32)

    def accumulate(carry, pair):
        total_a, total_b = carry
        token_rows = pair[0].astype(jnp.float32)
        grad_rows = pair[1].astype(jnp.float32)
        hidden = jnp.dot(token_rows, factor_a).astype(jnp.bfloat16).astype(jnp.float32)
        spread = lax.dot_general(grad_rows, factor_b, (((1,), (1,)), ((), ()))).astype(jnp.bfloat16).astype(jnp.float32)
        total_a = total_a + lax.dot_general(token_rows, spread, (((0,), (0,)), ((), ())))
        total_b = total_b + lax.dot_general(hidden, grad_rows, (((0,), (0,)), ((), ())))
        return (total_a, total_b), None

    start = (jnp.zeros((D, R), jnp.float32), jnp.zeros((R, KW), jnp.float32))
    totals, unused = lax.scan(accumulate, start, (token_blocks, grad_blocks))
    factor = TOKENS ** -0.5
    return totals[0] * factor, totals[1] * factor
```

```python
import functools
import math

import jax
import jax.numpy as jnp
from jax import lax
from jax.experimental import pallas as pl
from jax.experimental.pallas import tpu as pltpu
from jax.sharding import PartitionSpec as P

MESH = pl.DeviceIdType.MESH
BF16, F32 = jnp.bfloat16, jnp.float32


def dot(left, right, contract):
    return lax.dot_general(left, right, (contract, ((), ())), preferred_element_type=F32)


def kernel(sizes, tok_hbm, gk_hbm, a_ref, b_ref, oa_ref, ob_ref, *scratch):
    nz, ny, nd, pad, factor = sizes
    nblk = nz * ny
    tok, gk, spread, pb, load_sem = scratch[:5]
    half = (len(scratch) - 5) // 2
    names = ["g", "gzs", "gzr", "gys", "gyr", "gcs", "gcr", "pp", "sc", "rc", "rcs", "rcr"]
    names += ["sy", "ry", "rys", "ryr", "sz", "rz", "rzs", "rzr", "rx", "rxs", "rxr", "fin", "fs", "fr"]
    fam_a = dict(zip(names, scratch[5 : 5 + half]))
    fam_b = dict(zip(names, scratch[5 + half :]))
    rows_b = b_ref.shape[0]
    blk, dp = lax.axis_index("blk"), lax.axis_index("dp")
    z, y = lax.div(blk, ny), lax.rem(blk, ny)
    d, c = lax.div(dp, 2), lax.rem(dp, 2)
    peer = (blk, d * 2 + (1 - c))

    def near(zo, yo):
        return lax.rem(z + zo + nz, nz) * ny + lax.rem(y + yo + ny, ny)

    def away(xo):
        return lax.rem(d + xo + nd, nd)

    load_tok = pltpu.make_async_copy(tok_hbm, tok, load_sem.at[0])
    load_gk = pltpu.make_async_copy(gk_hbm, gk, load_sem.at[1])
    load_gk.start()
    load_tok.start()

    barrier = pltpu.get_barrier_semaphore()
    others = [(near(zo, 0), dp) for zo in range(1, nz)]
    others += [(near(0, yo), dp) for yo in range(1, ny)]
    others += [(blk, away(xo) * 2 + c) for xo in range(1, nd)] + [peer]
    for other in others:
        pl.semaphore_signal(barrier, inc=1, device_id=other, device_id_type=MESH)

    wide = fam_b["g"].shape[3]
    fam_b["g"][blk] = jnp.zeros(fam_b["g"].shape[1:], BF16)
    fam_b["g"][blk, 0, :rows_b] = b_ref[:, :wide]
    fam_b["g"][blk, 1, :rows_b] = b_ref[:, wide:]
    fam_a["g"][blk] = a_ref[...].T.reshape(fam_a["g"].shape[1:])
    pl.semaphore_wait(barrier, len(others))

    sent = []

    def rcopy(src, dst, ssem, rsem, device):
        return pltpu.make_async_remote_copy(
            src_ref=src, dst_ref=dst, send_sem=ssem, recv_sem=rsem,
            device_id=device, device_id_type=MESH,
        )

    def send(*args):
        copy = rcopy(*args)
        copy.start()
        sent.append(copy)

    def g_z(f, zo, at):
        part = f["g"].at[at, c]
        return part, part, f["gzs"].at[zo - 1], f["gzr"].at[zo - 1], (near(zo, 0), dp)

    def g_y(f, zo, yo, at):
        part = f["g"].at[at, c]
        return part, part, f["gys"].at[yo - 1, zo], f["gyr"].at[yo - 1, zo], (near(0, yo), dp)

    def g_c(f, zo, yo, at, side):
        k = yo * nz + zo - 1
        part = f["g"].at[at, side]
        return part, part, f["gcs"].at[k], f["gcr"].at[k], peer

    def gather_start(f):
        for zo in range(1, nz):
            send(*g_z(f, zo, blk))
        for yo in range(1, ny):
            send(*g_y(f, 0, yo, blk))

    def gather_z(f):
        for zo in range(1, nz):
            at = near(-zo, 0)
            rcopy(*g_z(f, zo, at)).wait_recv()
            for yo in range(1, ny):
                send(*g_y(f, zo, yo, at))
            send(*g_c(f, zo, 0, at, c))

    def gather_y(f):
        for zo in range(nz):
            for yo in range(1, ny):
                at = near(-zo, -yo)
                rcopy(*g_y(f, zo, yo, at)).wait_recv()
                send(*g_c(f, zo, yo, at, c))

    def gathered(f, zo, yo):
        at = near(-zo, -yo)
        if zo or yo:
            rcopy(*g_c(f, zo, yo, at, 1 - c)).wait_recv()
        return at

    def r_c(f, zo, yo):
        k = yo * nz + zo
        return f["sc"].at[k], f["rc"].at[k], f["rcs"].at[k], f["rcr"].at[k], peer

    def r_y(f, zo, yo):
        i = (yo - 1, zo)
        return f["sy"].at[i], f["ry"].at[i], f["rys"].at[i], f["ryr"].at[i], (near(0, yo), dp)

    def r_z(f, zo):
        i = zo - 1
        return f["sz"].at[i], f["rz"].at[i], f["rzs"].at[i], f["rzr"].at[i], (near(zo, 0), dp)

    def r_x(f, xo, at):
        part = f["rx"].at[at]
        return part, part, f["rxs"].at[xo - 1], f["rxr"].at[xo - 1], (blk, away(xo) * 2 + c)

    def r_f(f, side):
        part = f["fin"].at[side]
        return part, part, f["fs"], f["fr"], peer

    order = list(range(1, nz)) + [0]

    def reduce_start(f, zo, yo, mine, theirs):
        k = yo * nz + zo
        f["sc"][k] = theirs.astype(BF16)
        send(*r_c(f, zo, yo))
        f["pp"][k] = mine

    def chip_sum(f, zo, yo):
        k = yo * nz + zo
        rcopy(*r_c(f, zo, yo)).wait_recv()
        return f["pp"][k] + f["rc"][k].astype(F32)

    def reduce_y(f):
        for zo in order:
            for yo in range(1, ny):
                f["sy"][yo - 1, zo] = chip_sum(f, zo, yo).astype(BF16)
                send(*r_y(f, zo, yo))

    def reduce_z(f):
        for zo in order:
            total = chip_sum(f, zo, 0)
            for yo in range(1, ny):
                rcopy(*r_y(f, zo, yo)).wait_recv()
                total = total + f["ry"][yo - 1, zo].astype(F32)
            if zo:
                f["sz"][zo - 1] = total.astype(BF16)
                send(*r_z(f, zo))
            else:
                f["pp"][0] = total

    def reduce_x(f):
        total = f["pp"][0]
        for zo in range(1, nz):
            rcopy(*r_z(f, zo)).wait_recv()
            total = total + f["rz"][zo - 1].astype(F32)
        f["rx"][d] = total * factor
        for xo in range(1, nd):
            send(*r_x(f, xo, d))

    def reduce_last(f):
        for xo in range(1, nd):
            rcopy(*r_x(f, xo, away(-xo))).wait_recv()
        total = f["rx"][0]
        for at in range(1, nd):
            total = total + f["rx"][at]
        f["fin"][c] = total
        send(*r_f(f, c))

    def finish(f, out):
        rcopy(*r_f(f, 1 - c)).wait_recv()
        out[...] = f["fin"][...]

    gather_start(fam_b)
    gather_start(fam_a)
    gather_z(fam_b)
    gather_y(fam_b)

    rank = a_ref.shape[1]
    shape = (rank, nblk * pad)
    row, col = lax.broadcasted_iota(jnp.int32, shape, 0), lax.broadcasted_iota(jnp.int32, shape, 1)
    place = lax.rem(col, pad)
    pick = (row == lax.div(col, pad) * rows_b + place) & (place < rows_b)
    pick = jnp.where(pick, 1.0, 0.0).astype(BF16)
    gather_z(fam_a)
    for yo in range(ny):
        for zo in range(nz):
            gathered(fam_b, zo, yo)
    load_gk.wait()
    flow = jnp.zeros((rank, tok.shape[0]), F32)
    for s in range(2):
        factor_b = dot(pick, fam_b["g"][:, s].reshape(nblk * pad, wide), ((1,), (0,))).astype(BF16)
        flow = flow + dot(factor_b, gk[:, s * wide : (s + 1) * wide], ((1,), (1,)))
    spread[...] = flow.astype(BF16).reshape(spread.shape)
    both = jnp.concatenate([spread[c], spread[1 - c]], axis=0)

    cols = fam_a["g"].shape[3]

    def tok_part(at):
        return tok[:, pl.ds(pl.multiple_of(at * cols, cols), cols)]

    load_tok.wait()
    for yo in list(range(1, ny)) + [0]:
        for zo in order:
            part = dot(both, tok_part(near(zo, yo)), ((1,), (0,)))
            reduce_start(fam_a, zo, yo, part[: rank // 2], part[rank // 2 :])
    gather_y(fam_a)
    reduce_y(fam_a)
    hidden = jnp.zeros((rank, tok.shape[0]), F32)
    for yo in range(ny):
        for zo in range(nz):
            at = gathered(fam_a, zo, yo)
            hidden = hidden + dot(fam_a["g"][at].reshape(rank, cols), tok_part(at), ((1,), (1,)))
    hidden = dot(pick, hidden.astype(BF16), ((0,), (0,))).astype(BF16)
    pb[...] = dot(hidden, gk[...], ((1,), (0,)))
    for yo in list(range(1, ny)) + [0]:
        for zo in order:
            lines = pl.ds(pl.multiple_of(near(zo, yo) * pad, pad), pad)
            mine = pb[lines, pl.ds(pl.multiple_of(c * wide, wide), wide)]
            theirs = pb[lines, pl.ds(pl.multiple_of((1 - c) * wide, wide), wide)]
            reduce_start(fam_b, zo, yo, mine, theirs)
    reduce_z(fam_a)
    reduce_y(fam_b)
    reduce_z(fam_b)
    reduce_x(fam_a)
    reduce_x(fam_b)
    reduce_last(fam_a)
    reduce_last(fam_b)
    finish(fam_a, oa_ref)
    finish(fam_b, ob_ref)
    for copy in sent:
        copy.wait_send()


def family(nz, ny, nd, h, w):
    vm, dma = pltpu.VMEM, pltpu.SemaphoreType.DMA
    n = nz * ny
    return [
        vm((n, 2, h, w), BF16), dma((nz - 1,)), dma((nz - 1,)),
        dma((ny - 1, nz)), dma((ny - 1, nz)), dma((n - 1,)), dma((n - 1,)),
        vm((n, h, w), F32), vm((n, h, w), BF16), vm((n, h, w), BF16), dma((n,)), dma((n,)),
        vm((ny - 1, nz, h, w), BF16), vm((ny - 1, nz, h, w), BF16),
        dma((ny - 1, nz)), dma((ny - 1, nz)),
        vm((nz - 1, h, w), BF16), vm((nz - 1, h, w), BF16), dma((nz - 1,)), dma((nz - 1,)),
        vm((nd, h, w), F32), dma((nd - 1,)), dma((nd - 1,)),
        vm((2, h, w), F32), dma(()), dma(()),
    ]


def shards(tokens, grad_k, adapter_a, adapter_b):
    nblk, ndp = lax.axis_size("blk"), lax.axis_size("dp")
    ny = 2 ** (int(math.log2(nblk)) // 2)
    nz, nd = nblk // ny, ndp // 2
    rows_a, rank = adapter_a.shape
    rows_b, width = adapter_b.shape
    pad = -(-rows_b // 16) * 16
    count = tokens.shape[0]
    factor = 1.0 / math.sqrt(count * nblk * ndp)
    sizes_a, sizes_b = (rank // 2, rows_a), (pad, width // 2)
    vmem, anywhere = pl.BlockSpec(memory_space=pltpu.VMEM), pl.BlockSpec(memory_space=pl.ANY)
    out_a, out_b = pl.pallas_call(
        functools.partial(kernel, (nz, ny, nd, pad, factor)),
        out_shape=[jax.ShapeDtypeStruct((2, *s), F32) for s in (sizes_a, sizes_b)],
        in_specs=[anywhere, anywhere, vmem, vmem],
        out_specs=[vmem, vmem],
        scratch_shapes=[
            pltpu.VMEM(tokens.shape, BF16),
            pltpu.VMEM(grad_k.shape, BF16),
            pltpu.VMEM((2, rank // 2, count), BF16),
            pltpu.VMEM((nblk * pad, width), F32),
            pltpu.SemaphoreType.DMA((2,)),
            *family(nz, ny, nd, *sizes_a),
            *family(nz, ny, nd, *sizes_b),
        ],
        compiler_params=pltpu.CompilerParams(
            collective_id=0, has_side_effects=True, vmem_limit_bytes=52 * 2**20
        ),
        cost_estimate=pl.CostEstimate(
            flops=4 * count * rank * (tokens.shape[1] + width),
            bytes_accessed=2 * count * (tokens.shape[1] + width),
            transcendentals=0,
        ),
    )(tokens, grad_k, adapter_a, adapter_b)
    grad_a = out_a.reshape(rank, rows_a).T
    grad_b = jnp.concatenate([out_b[0, :rows_b], out_b[1, :rows_b]], axis=1)
    return grad_a, grad_b


def solution(mesh):
    return jax.shard_map(
        shards,
        mesh=mesh,
        in_specs=(P(("blk", "dp"), None), P(("blk", "dp"), None), P("blk", None), P("blk", None)),
        out_specs=(P("blk", None), P("blk", None)),
        check_vma=False,
    )
```

```python
import functools
import math

import jax
import jax.numpy as jnp
from jax import lax
from jax.experimental import pallas as pl
from jax.experimental.pallas import tpu as pltpu
from jax.sharding import PartitionSpec as P

MESH = pl.DeviceIdType.MESH
BF16, F32 = jnp.bfloat16, jnp.float32
HP = 48


def dot(left, right, contract):
    return lax.dot_general(left, right, (contract, ((), ())), preferred_element_type=F32)


def kernel(sizes, tok_hbm, gk_hbm, a_hbm, b_hbm, oa_ref, ob_ref, *scratch):
    nz, ny, nd, pad, hp, factor = sizes
    nblk = nz * ny
    tok, gk, own_b, spread, pb, load_sem = scratch[:6]
    half = 26
    names = ["g", "gzs", "gzr", "gys", "gyr", "gcs", "gcr", "pp", "sc", "rc", "rcs", "rcr"]
    names += ["sy", "ry", "rys", "ryr", "sz", "rz", "rzs", "rzr", "rx", "rxs", "rxr", "fin", "fs", "fr"]
    fam_a = dict(zip(names, scratch[6 : 6 + half]))
    fam_b = dict(zip(names, scratch[6 + half : 6 + 2 * half]))
    names_q = ["sx", "rx", "sxs", "rxr", "sy", "ry", "rys", "ryr", "sz", "rz", "rzs", "rzr"]
    fam_q = dict(zip(names_q + ["fin", "fs", "fr"], scratch[6 + 2 * half :]))
    rows_b = b_hbm.shape[0]
    blk, dp = lax.axis_index("blk"), lax.axis_index("dp")
    z, y = lax.div(blk, ny), lax.rem(blk, ny)
    d, c = lax.div(dp, 2), lax.rem(dp, 2)
    peer = (blk, d * 2 + (1 - c))
    across = (blk, (1 - d) * 2 + c)

    def near(zo, yo):
        return lax.rem(z + zo + nz, nz) * ny + lax.rem(y + yo + ny, ny)

    def away(xo):
        return lax.rem(d + xo + nd, nd)

    load_tok = pltpu.make_async_copy(tok_hbm, tok, load_sem.at[0])
    load_gk = pltpu.make_async_copy(gk_hbm, gk, load_sem.at[1])
    load_a = pltpu.make_async_copy(a_hbm, fam_a["g"].at[blk], load_sem.at[2])
    load_b = pltpu.make_async_copy(b_hbm, own_b, load_sem.at[3])
    for load in (load_b, load_a, load_gk, load_tok):
        load.start()

    barrier = pltpu.get_barrier_semaphore()
    others = [(near(zo, 0), dp) for zo in range(1, nz)]
    others += [(near(0, yo), dp) for yo in range(1, ny)]
    others += [(blk, away(xo) * 2 + c) for xo in range(1, nd)] + [peer]
    for other in others:
        pl.semaphore_signal(barrier, inc=1, device_id=other, device_id_type=MESH)

    wide = fam_b["g"].shape[3]
    fam_b["g"][blk] = jnp.zeros(fam_b["g"].shape[1:], BF16)
    load_b.wait()
    fam_b["g"][blk, 0, :rows_b] = own_b[:, :wide]
    fam_b["g"][blk, 1, :rows_b] = own_b[:, wide:]
    load_a.wait()
    pl.semaphore_wait(barrier, len(others))

    sent = []

    def rcopy(src, dst, ssem, rsem, device):
        return pltpu.make_async_remote_copy(
            src_ref=src, dst_ref=dst, send_sem=ssem, recv_sem=rsem,
            device_id=device, device_id_type=MESH,
        )

    def send(*args):
        copy = rcopy(*args)
        copy.start()
        sent.append(copy)

    def g_z(f, zo, at):
        part = f["g"].at[at, c]
        return part, part, f["gzs"].at[zo - 1], f["gzr"].at[zo - 1], (near(zo, 0), dp)

    def g_y(f, zo, yo, at):
        part = f["g"].at[at, c]
        return part, part, f["gys"].at[yo - 1, zo], f["gyr"].at[yo - 1, zo], (near(0, yo), dp)

    def g_c(f, zo, yo, at, side):
        k = yo * nz + zo - 1
        part = f["g"].at[at, side]
        return part, part, f["gcs"].at[k], f["gcr"].at[k], peer

    def gather_start(f):
        for zo in range(1, nz):
            send(*g_z(f, zo, blk))
        for yo in range(1, ny):
            send(*g_y(f, 0, yo, blk))

    def gather_z(f):
        for zo in range(1, nz):
            at = near(-zo, 0)
            rcopy(*g_z(f, zo, at)).wait_recv()
            for yo in range(1, ny):
                send(*g_y(f, zo, yo, at))
            send(*g_c(f, zo, 0, at, c))

    def gather_y(f):
        for zo in range(nz):
            for yo in range(1, ny):
                at = near(-zo, -yo)
                rcopy(*g_y(f, zo, yo, at)).wait_recv()
                send(*g_c(f, zo, yo, at, c))

    def gathered(f, zo, yo):
        at = near(-zo, -yo)
        if zo or yo:
            rcopy(*g_c(f, zo, yo, at, 1 - c)).wait_recv()
        return at

    def r_c(f, zo, yo):
        k = yo * nz + zo
        return f["sc"].at[k], f["rc"].at[k], f["rcs"].at[k], f["rcr"].at[k], peer

    def r_y(f, zo, yo):
        i = (yo - 1, zo)
        return f["sy"].at[i], f["ry"].at[i], f["rys"].at[i], f["ryr"].at[i], (near(0, yo), dp)

    def r_z(f, zo):
        i = zo - 1
        return f["sz"].at[i], f["rz"].at[i], f["rzs"].at[i], f["rzr"].at[i], (near(zo, 0), dp)

    def r_x(f, xo, at):
        part = f["rx"].at[at]
        return part, part, f["rxs"].at[xo - 1], f["rxr"].at[xo - 1], (blk, away(xo) * 2 + c)

    def r_f(f, side):
        part = f["fin"].at[side]
        return part, part, f["fs"], f["fr"], peer

    order = list(range(1, nz)) + [0]

    def reduce_start(f, zo, yo, mine, theirs):
        k = yo * nz + zo
        f["sc"][k] = theirs.astype(BF16)
        send(*r_c(f, zo, yo))
        f["pp"][k] = mine

    def chip_sum(f, zo, yo):
        k = yo * nz + zo
        rcopy(*r_c(f, zo, yo)).wait_recv()
        return f["pp"][k] + f["rc"][k].astype(F32)

    def reduce_y(f):
        for zo in order:
            for yo in range(1, ny):
                f["sy"][yo - 1, zo] = chip_sum(f, zo, yo).astype(BF16)
                send(*r_y(f, zo, yo))

    def reduce_z(f):
        for zo in order:
            total = chip_sum(f, zo, 0)
            for yo in range(1, ny):
                rcopy(*r_y(f, zo, yo)).wait_recv()
                total = total + f["ry"][yo - 1, zo].astype(F32)
            if zo:
                f["sz"][zo - 1] = total.astype(BF16)
                send(*r_z(f, zo))
            else:
                f["pp"][0] = total

    def q_x(k):
        return fam_q["sx"].at[k], fam_q["rx"].at[k], fam_q["sxs"].at[k], fam_q["rxr"].at[k], across

    def q_last(at):
        part = fam_q["fin"].at[at]
        return part, part, fam_q["fs"], fam_q["fr"], across

    def cols_of(at):
        narrow = fam_a["pp"].shape[2] // 2
        return pl.ds(pl.multiple_of(at * narrow, narrow), narrow)

    def spread_out(f, zo, yo):
        k = yo * nz + zo
        f["pp"][k] = chip_sum(f, zo, yo)
        if fam_q:
            fam_q["sx"][k] = f["pp"][k, hp:, cols_of(1 - d)].astype(BF16)
            send(*q_x(k))
        if yo:
            f["sy"][yo - 1, zo] = f["pp"][k, :hp].astype(BF16)
            send(*r_y(f, zo, yo))

    def q_sum(zo, yo):
        k = yo * nz + zo
        rcopy(*q_x(k)).wait_recv()
        return fam_a["pp"][k, hp:, cols_of(d)] + fam_q["rx"][k].astype(F32)

    def y_sum(f, zo, total):
        for yo in range(1, ny):
            rcopy(*r_y(f, zo, yo)).wait_recv()
            total = total + f["ry"][yo - 1, zo].astype(F32)
        if zo:
            f["sz"][zo - 1] = total.astype(BF16)
            send(*r_z(f, zo))
        return total

    def z_sum(f, total):
        for zo in range(1, nz):
            rcopy(*r_z(f, zo)).wait_recv()
            total = total + f["rz"][zo - 1].astype(F32)
        return total * factor

    def reduce_x(f):
        total = f["pp"][0]
        for zo in range(1, nz):
            rcopy(*r_z(f, zo)).wait_recv()
            total = total + f["rz"][zo - 1].astype(F32)
        f["rx"][d] = total * factor
        for xo in range(1, nd):
            send(*r_x(f, xo, d))

    def reduce_last(f):
        for xo in range(1, nd):
            rcopy(*r_x(f, xo, away(-xo))).wait_recv()
        total = f["rx"][0]
        for at in range(1, nd):
            total = total + f["rx"][at]
        f["fin"][c] = total
        send(*r_f(f, c))

    def finish(f, out):
        rcopy(*r_f(f, 1 - c)).wait_recv()
        out[...] = f["fin"][...]

    gather_start(fam_b)
    gather_start(fam_a)
    gather_z(fam_b)
    gather_y(fam_b)

    rank = 2 * a_hbm.shape[1]
    shape = (rank, nblk * pad)
    row, col = lax.broadcasted_iota(jnp.int32, shape, 0), lax.broadcasted_iota(jnp.int32, shape, 1)
    place = lax.rem(col, pad)
    pick = (row == lax.div(col, pad) * rows_b + place) & (place < rows_b)
    pick = jnp.where(pick, 1.0, 0.0).astype(BF16)
    gather_z(fam_a)
    for yo in range(ny):
        for zo in range(nz):
            gathered(fam_b, zo, yo)
    load_gk.wait()
    flow = jnp.zeros((rank, tok.shape[0]), F32)
    for s in range(2):
        factor_b = dot(pick, fam_b["g"][:, s].reshape(nblk * pad, wide), ((1,), (0,))).astype(BF16)
        flow = flow + dot(factor_b, gk[:, s * wide : (s + 1) * wide], ((1,), (1,)))
    spread[...] = flow.astype(BF16).reshape(spread.shape)
    both = jnp.concatenate([spread[c], spread[1 - c]], axis=0)

    cols = fam_a["g"].shape[3]

    def tok_part(at):
        return tok[:, pl.ds(pl.multiple_of(at * cols, cols), cols)]

    load_tok.wait()
    for yo in list(range(1, ny)) + [0]:
        for zo in order:
            part = dot(both, tok_part(near(zo, yo)), ((1,), (0,)))
            reduce_start(fam_a, zo, yo, part[: rank // 2], part[rank // 2 :])
    gather_y(fam_a)
    for yo in [*range(1, ny), 0]:
        for zo in order:
            spread_out(fam_a, zo, yo)
    if fam_q:
        for zo in order:
            for yo in range(1, ny):
                fam_q["sy"][yo - 1, zo] = q_sum(zo, yo).astype(BF16)
                send(*r_y(fam_q, zo, yo))
    hidden = jnp.zeros((rank, tok.shape[0]), F32)
    for yo in range(ny):
        for zo in range(nz):
            at = gathered(fam_a, zo, yo)
            hidden = hidden + dot(fam_a["g"][at].reshape(rank, cols), tok_part(at), ((1,), (1,)))
    hidden = dot(pick, hidden.astype(BF16), ((0,), (0,))).astype(BF16)
    pb[...] = dot(hidden, gk[...], ((1,), (0,)))
    for yo in list(range(1, ny)) + [0]:
        for zo in order:
            lines = pl.ds(pl.multiple_of(near(zo, yo) * pad, pad), pad)
            mine = pb[lines, pl.ds(pl.multiple_of(c * wide, wide), wide)]
            theirs = pb[lines, pl.ds(pl.multiple_of((1 - c) * wide, wide), wide)]
            reduce_start(fam_b, zo, yo, mine, theirs)
    for zo in order:
        own = y_sum(fam_a, zo, fam_a["pp"][zo, :hp])
    if fam_q:
        for zo in order:
            own_q = y_sum(fam_q, zo, q_sum(zo, 0))
    reduce_y(fam_b)
    reduce_z(fam_b)
    fam_a["rx"][d] = z_sum(fam_a, own)
    for xo in range(1, nd):
        send(*r_x(fam_a, xo, d))
    if fam_q:
        fam_q["fin"][d] = z_sum(fam_q, own_q)
        send(*q_last(d))
    reduce_x(fam_b)
    for xo in range(1, nd):
        rcopy(*r_x(fam_a, xo, away(-xo))).wait_recv()
    total = fam_a["rx"][0]
    for at in range(1, nd):
        total = total + fam_a["rx"][at]
    fam_a["fin"][c, :hp] = total
    if fam_q:
        rcopy(*q_last(1 - d)).wait_recv()
        narrow = cols // 2
        fam_a["fin"][c, hp:, :narrow] = fam_q["fin"][0]
        fam_a["fin"][c, hp:, narrow:] = fam_q["fin"][1]
    send(*r_f(fam_a, c))
    reduce_last(fam_b)
    finish(fam_a, oa_ref)
    finish(fam_b, ob_ref)
    for copy in sent:
        copy.wait_send()


def family(nz, ny, nd, h, w, hp):
    vm, dma = pltpu.VMEM, pltpu.SemaphoreType.DMA
    n = nz * ny
    return [
        vm((n, 2, h, w), BF16), dma((nz - 1,)), dma((nz - 1,)),
        dma((ny - 1, nz)), dma((ny - 1, nz)), dma((n - 1,)), dma((n - 1,)),
        vm((n, h, w), F32), vm((n, h, w), BF16), vm((n, h, w), BF16), dma((n,)), dma((n,)),
        vm((ny - 1, nz, hp, w), BF16), vm((ny - 1, nz, hp, w), BF16),
        dma((ny - 1, nz)), dma((ny - 1, nz)),
        vm((nz - 1, hp, w), BF16), vm((nz - 1, hp, w), BF16), dma((nz - 1,)), dma((nz - 1,)),
        vm((nd, hp, w), F32), dma((nd - 1,)), dma((nd - 1,)),
        vm((2, h, w), F32), dma(()), dma(()),
    ]


def family_q(nz, ny, h, w):
    vm, dma = pltpu.VMEM, pltpu.SemaphoreType.DMA
    n = nz * ny
    return [
        vm((n, h, w), BF16), vm((n, h, w), BF16), dma((n,)), dma((n,)),
        vm((ny - 1, nz, h, w), BF16), vm((ny - 1, nz, h, w), BF16),
        dma((ny - 1, nz)), dma((ny - 1, nz)),
        vm((nz - 1, h, w), BF16), vm((nz - 1, h, w), BF16), dma((nz - 1,)), dma((nz - 1,)),
        vm((2, h, w), F32), dma(()), dma(()),
    ]


def shards(tokens, grad_k, adapter_a, adapter_b):
    nblk, ndp = lax.axis_size("blk"), lax.axis_size("dp")
    ny = 2 ** (int(math.log2(nblk)) // 2)
    nz, nd = nblk // ny, ndp // 2
    rows_a, rank = adapter_a.shape
    rows_b, width = adapter_b.shape
    pad = -(-rows_b // 16) * 16
    count = tokens.shape[0]
    factor = 1.0 / math.sqrt(count * nblk * ndp)
    sizes_a, sizes_b = (rank // 2, rows_a), (pad, width // 2)
    two = nd == 2 and rank % 64 == 0 and rows_a % 256 == 0
    hp = HP if two else rank // 2
    second = family_q(nz, ny, rank // 2 - hp, rows_a // 2) if two else []
    vmem, anywhere = pl.BlockSpec(memory_space=pltpu.VMEM), pl.BlockSpec(memory_space=pl.ANY)
    out_a, out_b = pl.pallas_call(
        functools.partial(kernel, (nz, ny, nd, pad, hp, factor)),
        out_shape=[jax.ShapeDtypeStruct((2, *s), F32) for s in (sizes_a, sizes_b)],
        in_specs=[anywhere] * 4,
        out_specs=[vmem, vmem],
        scratch_shapes=[
            pltpu.VMEM(tokens.shape, BF16),
            pltpu.VMEM(grad_k.shape, BF16),
            pltpu.VMEM(adapter_b.shape, BF16),
            pltpu.VMEM((2, rank // 2, count), BF16),
            pltpu.VMEM((nblk * pad, width), F32),
            pltpu.SemaphoreType.DMA((4,)),
            *family(nz, ny, nd, *sizes_a, hp),
            *family(nz, ny, nd, *sizes_b, pad),
            *second,
        ],
        compiler_params=pltpu.CompilerParams(
            collective_id=0, has_side_effects=True, vmem_limit_bytes=62 * 2**20
        ),
        cost_estimate=pl.CostEstimate(
            flops=4 * count * rank * (tokens.shape[1] + width),
            bytes_accessed=2 * count * (tokens.shape[1] + width),
            transcendentals=0,
        ),
    )(tokens, grad_k, adapter_a.T.reshape(2, rank // 2, rows_a), adapter_b)
    grad_a = out_a.reshape(rank, rows_a).T
    grad_b = jnp.concatenate([out_b[0, :rows_b], out_b[1, :rows_b]], axis=1)
    return grad_a, grad_b


def solution(mesh):
    return jax.shard_map(
        shards,
        mesh=mesh,
        in_specs=(P(("blk", "dp"), None), P(("blk", "dp"), None), P("blk", None), P("blk", None)),
        out_specs=(P("blk", None), P("blk", None)),
        check_vma=False,
    )
```

```python
import functools
import math

import jax
import jax.numpy as jnp
from jax import lax
from jax.experimental import pallas as pl
from jax.experimental.pallas import tpu as pltpu
from jax.sharding import PartitionSpec as P

MESH = pl.DeviceIdType.MESH
BF16, F32 = jnp.bfloat16, jnp.float32
HP = 48


def dot(left, right, contract):
    return lax.dot_general(left, right, (contract, ((), ())), preferred_element_type=F32)


def kernel(sizes, tok_hbm, gk_hbm, a_hbm, b_hbm, oa_ref, ob_ref, *scratch):
    nz, ny, nd, pad, hp, factor = sizes
    nblk = nz * ny
    tok, gk, own_b, spread, pb, load_sem = scratch[:6]
    half = 26
    names = ["g", "gzs", "gzr", "gys", "gyr", "gcs", "gcr", "pp", "sc", "rc", "rcs", "rcr"]
    names += ["sy", "ry", "rys", "ryr", "sz", "rz", "rzs", "rzr", "rx", "rxs", "rxr", "fin", "fs", "fr"]
    fam_a = dict(zip(names, scratch[6 : 6 + half]))
    fam_b = dict(zip(names, scratch[6 + half : 6 + 2 * half]))
    names_q = ["sx", "rx", "sxs", "rxr", "sy", "ry", "rys", "ryr", "sz", "rz", "rzs", "rzr"]
    fam_q = dict(zip(names_q + ["fin", "fs", "fr"], scratch[6 + 2 * half :]))
    rows_b = b_hbm.shape[0]
    blk, dp = lax.axis_index("blk"), lax.axis_index("dp")
    z, y = lax.div(blk, ny), lax.rem(blk, ny)
    d, c = lax.div(dp, 2), lax.rem(dp, 2)
    peer = (blk, d * 2 + (1 - c))
    across = (blk, (1 - d) * 2 + c)

    def near(zo, yo):
        return lax.rem(z + zo + nz, nz) * ny + lax.rem(y + yo + ny, ny)

    def away(xo):
        return lax.rem(d + xo + nd, nd)

    load_tok = pltpu.make_async_copy(tok_hbm, tok, load_sem.at[0])
    load_gk = pltpu.make_async_copy(gk_hbm, gk, load_sem.at[1])
    load_a = pltpu.make_async_copy(a_hbm, fam_a["g"].at[blk], load_sem.at[2])
    load_b = pltpu.make_async_copy(b_hbm, own_b, load_sem.at[3])
    for load in (load_b, load_a, load_gk, load_tok):
        load.start()

    barrier = pltpu.get_barrier_semaphore()
    others = [(near(zo, 0), dp) for zo in range(1, nz)]
    others += [(near(0, yo), dp) for yo in range(1, ny)]
    others += [(blk, away(xo) * 2 + c) for xo in range(1, nd)] + [peer]
    for other in others:
        pl.semaphore_signal(barrier, inc=1, device_id=other, device_id_type=MESH)

    wide = fam_b["g"].shape[3]
    fam_b["g"][blk] = jnp.zeros(fam_b["g"].shape[1:], BF16)
    load_b.wait()
    fam_b["g"][blk, 0, :rows_b] = own_b[:, :wide]
    fam_b["g"][blk, 1, :rows_b] = own_b[:, wide:]
    load_a.wait()
    pl.semaphore_wait(barrier, len(others))

    sent = []

    def rcopy(src, dst, ssem, rsem, device):
        return pltpu.make_async_remote_copy(
            src_ref=src, dst_ref=dst, send_sem=ssem, recv_sem=rsem,
            device_id=device, device_id_type=MESH,
        )

    def send(*args):
        copy = rcopy(*args)
        copy.start()
        sent.append(copy)

    def g_z(f, zo, at):
        part = f["g"].at[at, c]
        return part, part, f["gzs"].at[zo - 1], f["gzr"].at[zo - 1], (near(zo, 0), dp)

    def g_y(f, zo, yo, at):
        part = f["g"].at[at, c]
        return part, part, f["gys"].at[yo - 1, zo], f["gyr"].at[yo - 1, zo], (near(0, yo), dp)

    def g_c(f, zo, yo, at, side):
        k = yo * nz + zo - 1
        part = f["g"].at[at, side]
        return part, part, f["gcs"].at[k], f["gcr"].at[k], peer

    def gather_start(f):
        for zo in range(1, nz):
            send(*g_z(f, zo, blk))
        for yo in range(1, ny):
            send(*g_y(f, 0, yo, blk))

    def gather_z(f):
        for zo in range(1, nz):
            at = near(-zo, 0)
            rcopy(*g_z(f, zo, at)).wait_recv()
            for yo in range(1, ny):
                send(*g_y(f, zo, yo, at))
            send(*g_c(f, zo, 0, at, c))

    def gather_y(f):
        for zo in range(nz):
            for yo in range(1, ny):
                at = near(-zo, -yo)
                rcopy(*g_y(f, zo, yo, at)).wait_recv()
                send(*g_c(f, zo, yo, at, c))

    def gathered(f, zo, yo):
        at = near(-zo, -yo)
        if zo or yo:
            rcopy(*g_c(f, zo, yo, at, 1 - c)).wait_recv()
        return at

    def r_c(f, zo, yo):
        k = yo * nz + zo
        return f["sc"].at[k], f["rc"].at[k], f["rcs"].at[k], f["rcr"].at[k], peer

    def r_y(f, zo, yo):
        i = (yo - 1, zo)
        return f["sy"].at[i], f["ry"].at[i], f["rys"].at[i], f["ryr"].at[i], (near(0, yo), dp)

    def r_z(f, zo):
        i = zo - 1
        return f["sz"].at[i], f["rz"].at[i], f["rzs"].at[i], f["rzr"].at[i], (near(zo, 0), dp)

    def r_x(f, xo, at):
        part = f["rx"].at[at]
        return part, part, f["rxs"].at[xo - 1], f["rxr"].at[xo - 1], (blk, away(xo) * 2 + c)

    def r_f(f, side):
        part = f["fin"].at[side]
        return part, part, f["fs"], f["fr"], peer

    order = list(range(1, nz)) + [0]

    def reduce_start(f, zo, yo, mine, theirs):
        k = yo * nz + zo
        f["sc"][k] = theirs.astype(BF16)
        send(*r_c(f, zo, yo))
        f["pp"][k] = mine

    def chip_sum(f, zo, yo):
        k = yo * nz + zo
        rcopy(*r_c(f, zo, yo)).wait_recv()
        return f["pp"][k] + f["rc"][k].astype(F32)

    def reduce_y(f):
        for zo in order:
            for yo in range(1, ny):
                f["sy"][yo - 1, zo] = chip_sum(f, zo, yo).astype(BF16)
                send(*r_y(f, zo, yo))

    def reduce_z(f):
        for zo in order:
            total = chip_sum(f, zo, 0)
            for yo in range(1, ny):
                rcopy(*r_y(f, zo, yo)).wait_recv()
                total = total + f["ry"][yo - 1, zo].astype(F32)
            if zo:
                f["sz"][zo - 1] = total.astype(BF16)
                send(*r_z(f, zo))
            else:
                f["pp"][0] = total

    def q_x(k):
        return fam_q["sx"].at[k], fam_q["rx"].at[k], fam_q["sxs"].at[k], fam_q["rxr"].at[k], across

    def q_last(at):
        part = fam_q["fin"].at[at]
        return part, part, fam_q["fs"], fam_q["fr"], across

    def cols_of(at):
        narrow = fam_a["pp"].shape[2] // 2
        return pl.ds(pl.multiple_of(at * narrow, narrow), narrow)

    def spread_out(f, zo, yo):
        k = yo * nz + zo
        f["pp"][k] = chip_sum(f, zo, yo)
        if fam_q:
            fam_q["sx"][k] = f["pp"][k, hp:, cols_of(1 - d)].astype(BF16)
            send(*q_x(k))
        if yo:
            f["sy"][yo - 1, zo] = f["pp"][k, :hp].astype(BF16)
            send(*r_y(f, zo, yo))

    def q_sum(zo, yo):
        k = yo * nz + zo
        rcopy(*q_x(k)).wait_recv()
        return fam_a["pp"][k, hp:, cols_of(d)] + fam_q["rx"][k].astype(F32)

    def y_sum(f, zo, total):
        for yo in range(1, ny):
            rcopy(*r_y(f, zo, yo)).wait_recv()
            total = total + f["ry"][yo - 1, zo].astype(F32)
        if zo:
            f["sz"][zo - 1] = total.astype(BF16)
            send(*r_z(f, zo))
        return total

    def z_sum(f, total):
        for zo in range(1, nz):
            rcopy(*r_z(f, zo)).wait_recv()
            total = total + f["rz"][zo - 1].astype(F32)
        return total * factor

    def reduce_x(f):
        total = f["pp"][0]
        for zo in range(1, nz):
            rcopy(*r_z(f, zo)).wait_recv()
            total = total + f["rz"][zo - 1].astype(F32)
        f["rx"][d] = total * factor
        for xo in range(1, nd):
            send(*r_x(f, xo, d))

    def reduce_last(f):
        for xo in range(1, nd):
            rcopy(*r_x(f, xo, away(-xo))).wait_recv()
        total = f["rx"][0]
        for at in range(1, nd):
            total = total + f["rx"][at]
        f["fin"][c] = total
        send(*r_f(f, c))

    def finish(f, out):
        rcopy(*r_f(f, 1 - c)).wait_recv()
        out[...] = f["fin"][...]

    gather_start(fam_b)
    gather_start(fam_a)
    gather_z(fam_b)
    gather_y(fam_b)

    rank = 2 * a_hbm.shape[1]
    shape = (rank, nblk * pad)
    row, col = lax.broadcasted_iota(jnp.int32, shape, 0), lax.broadcasted_iota(jnp.int32, shape, 1)
    place = lax.rem(col, pad)
    pick = (row == lax.div(col, pad) * rows_b + place) & (place < rows_b)
    pick = jnp.where(pick, 1.0, 0.0).astype(BF16)
    gather_z(fam_a)
    for yo in range(ny):
        for zo in range(nz):
            gathered(fam_b, zo, yo)
    load_gk.wait()
    flow = jnp.zeros((rank, tok.shape[0]), F32)
    for s in range(2):
        factor_b = dot(pick, fam_b["g"][:, s].reshape(nblk * pad, wide), ((1,), (0,))).astype(BF16)
        flow = flow + dot(factor_b, gk[:, s * wide : (s + 1) * wide], ((1,), (1,)))
    spread[...] = flow.astype(BF16).reshape(spread.shape)
    both = jnp.concatenate([spread[c], spread[1 - c]], axis=0)

    cols = fam_a["g"].shape[3]

    def tok_part(at):
        return tok[:, pl.ds(pl.multiple_of(at * cols, cols), cols)]

    load_tok.wait()
    for yo in list(range(1, ny)) + [0]:
        for zo in order:
            part = dot(both, tok_part(near(zo, yo)), ((1,), (0,)))
            reduce_start(fam_a, zo, yo, part[: rank // 2], part[rank // 2 :])
    for yo in [*range(1, ny), 0]:
        for zo in order:
            spread_out(fam_a, zo, yo)
    gather_y(fam_a)
    if fam_q:
        for zo in order:
            for yo in range(1, ny):
                fam_q["sy"][yo - 1, zo] = q_sum(zo, yo).astype(BF16)
                send(*r_y(fam_q, zo, yo))
    hidden = jnp.zeros((rank, tok.shape[0]), F32)
    for yo in range(ny):
        for zo in range(nz):
            at = gathered(fam_a, zo, yo)
            hidden = hidden + dot(fam_a["g"][at].reshape(rank, cols), tok_part(at), ((1,), (1,)))
    hidden = dot(pick, hidden.astype(BF16), ((0,), (0,))).astype(BF16)
    pb[...] = dot(hidden, gk[...], ((1,), (0,)))
    for yo in list(range(1, ny)) + [0]:
        for zo in order:
            lines = pl.ds(pl.multiple_of(near(zo, yo) * pad, pad), pad)
            mine = pb[lines, pl.ds(pl.multiple_of(c * wide, wide), wide)]
            theirs = pb[lines, pl.ds(pl.multiple_of((1 - c) * wide, wide), wide)]
            reduce_start(fam_b, zo, yo, mine, theirs)
    for zo in order:
        own = y_sum(fam_a, zo, fam_a["pp"][zo, :hp])
    if fam_q:
        for zo in order:
            own_q = y_sum(fam_q, zo, q_sum(zo, 0))
    reduce_y(fam_b)
    reduce_z(fam_b)
    fam_a["rx"][d] = z_sum(fam_a, own)
    for xo in range(1, nd):
        send(*r_x(fam_a, xo, d))
    if fam_q:
        fam_q["fin"][d] = z_sum(fam_q, own_q)
        send(*q_last(d))
    reduce_x(fam_b)
    for xo in range(1, nd):
        rcopy(*r_x(fam_a, xo, away(-xo))).wait_recv()
    total = fam_a["rx"][0]
    for at in range(1, nd):
        total = total + fam_a["rx"][at]
    fam_a["fin"][c, :hp] = total
    if fam_q:
        rcopy(*q_last(1 - d)).wait_recv()
        narrow = cols // 2
        fam_a["fin"][c, hp:, :narrow] = fam_q["fin"][0]
        fam_a["fin"][c, hp:, narrow:] = fam_q["fin"][1]
    send(*r_f(fam_a, c))
    reduce_last(fam_b)
    finish(fam_a, oa_ref)
    finish(fam_b, ob_ref)
    for copy in sent:
        copy.wait_send()


def family(nz, ny, nd, h, w, hp):
    vm, dma = pltpu.VMEM, pltpu.SemaphoreType.DMA
    n = nz * ny
    return [
        vm((n, 2, h, w), BF16), dma((nz - 1,)), dma((nz - 1,)),
        dma((ny - 1, nz)), dma((ny - 1, nz)), dma((n - 1,)), dma((n - 1,)),
        vm((n, h, w), F32), vm((n, h, w), BF16), vm((n, h, w), BF16), dma((n,)), dma((n,)),
        vm((ny - 1, nz, hp, w), BF16), vm((ny - 1, nz, hp, w), BF16),
        dma((ny - 1, nz)), dma((ny - 1, nz)),
        vm((nz - 1, hp, w), BF16), vm((nz - 1, hp, w), BF16), dma((nz - 1,)), dma((nz - 1,)),
        vm((nd, hp, w), F32), dma((nd - 1,)), dma((nd - 1,)),
        vm((2, h, w), F32), dma(()), dma(()),
    ]


def family_q(nz, ny, h, w):
    vm, dma = pltpu.VMEM, pltpu.SemaphoreType.DMA
    n = nz * ny
    return [
        vm((n, h, w), BF16), vm((n, h, w), BF16), dma((n,)), dma((n,)),
        vm((ny - 1, nz, h, w), BF16), vm((ny - 1, nz, h, w), BF16),
        dma((ny - 1, nz)), dma((ny - 1, nz)),
        vm((nz - 1, h, w), BF16), vm((nz - 1, h, w), BF16), dma((nz - 1,)), dma((nz - 1,)),
        vm((2, h, w), F32), dma(()), dma(()),
    ]


def shards(tokens, grad_k, adapter_a, adapter_b):
    nblk, ndp = lax.axis_size("blk"), lax.axis_size("dp")
    ny = 2 ** (int(math.log2(nblk)) // 2)
    nz, nd = nblk // ny, ndp // 2
    rows_a, rank = adapter_a.shape
    rows_b, width = adapter_b.shape
    pad = -(-rows_b // 16) * 16
    count = tokens.shape[0]
    factor = 1.0 / math.sqrt(count * nblk * ndp)
    sizes_a, sizes_b = (rank // 2, rows_a), (pad, width // 2)
    two = nd == 2 and rank % 64 == 0 and rows_a % 256 == 0
    hp = HP if two else rank // 2
    second = family_q(nz, ny, rank // 2 - hp, rows_a // 2) if two else []
    vmem, anywhere = pl.BlockSpec(memory_space=pltpu.VMEM), pl.BlockSpec(memory_space=pl.ANY)
    out_a, out_b = pl.pallas_call(
        functools.partial(kernel, (nz, ny, nd, pad, hp, factor)),
        out_shape=[jax.ShapeDtypeStruct((2, *s), F32) for s in (sizes_a, sizes_b)],
        in_specs=[anywhere] * 4,
        out_specs=[vmem, vmem],
        scratch_shapes=[
            pltpu.VMEM(tokens.shape, BF16),
            pltpu.VMEM(grad_k.shape, BF16),
            pltpu.VMEM(adapter_b.shape, BF16),
            pltpu.VMEM((2, rank // 2, count), BF16),
            pltpu.VMEM((nblk * pad, width), F32),
            pltpu.SemaphoreType.DMA((4,)),
            *family(nz, ny, nd, *sizes_a, hp),
            *family(nz, ny, nd, *sizes_b, pad),
            *second,
        ],
        compiler_params=pltpu.CompilerParams(
            collective_id=0, has_side_effects=True, vmem_limit_bytes=62 * 2**20
        ),
        cost_estimate=pl.CostEstimate(
            flops=4 * count * rank * (tokens.shape[1] + width),
            bytes_accessed=2 * count * (tokens.shape[1] + width),
            transcendentals=0,
        ),
    )(tokens, grad_k, adapter_a.T.reshape(2, rank // 2, rows_a), adapter_b)
    grad_a = out_a.reshape(rank, rows_a).T
    grad_b = jnp.concatenate([out_b[0, :rows_b], out_b[1, :rows_b]], axis=1)
    return grad_a, grad_b


def solution(mesh):
    return jax.shard_map(
        shards,
        mesh=mesh,
        in_specs=(P(("blk", "dp"), None), P(("blk", "dp"), None), P("blk", None), P("blk", None)),
        out_specs=(P("blk", None), P("blk", None)),
        check_vma=False,
    )
```
